512 devices in a mesh: pas: 64 (over z, y), qry: 8 (over x, core).
Axes of the slice: x: 4, y: 8, z: 8, core: 2. Of those that a mesh axis runs over, the one named last changes fastest.
Arguments:
- queries: bfloat16 [65536, 4096], P(('pas', 'qry')), as said below
- grad_out: bfloat16 [65536, 4096], P(('pas', 'qry')), may hold values from -6 to 6
- suffix_keys: bfloat16 [65536, 512], P(('pas', 'qry')), may hold values from -6 to 6
- suffix_values: bfloat16 [65536, 512], P(('pas', 'qry')), may hold values from -6 to 6
- passage_keys: bfloat16 [1024, 4, 512], P('pas'), as said below
- passage_values: bfloat16 [1024, 4, 512], P('pas'), may hold values from -6 to 6
- passage_lengths: int32 [1024], P('pas'), may hold values from 1 to 4
- retrieved: int32 [1024, 32], P(('pas', 'qry')), may hold values from 0 to 1023, as said below
Outputs:
- grad_queries: bfloat16 [65536, 4096], P(('pas', 'qry'))
- grad_suffix_keys: bfloat16 [65536, 512], P(('pas', 'qry'))
- grad_suffix_values: bfloat16 [65536, 512], P(('pas', 'qry'))
- grad_passage_keys: bfloat16 [1024, 4, 512], P(('pas', 'qry'))
- grad_passage_values: bfloat16 [1024, 4, 512], P(('pas', 'qry'))
The draws below stay inside these ranges and needn't reach their ends.
Inputs may be any that keep to these rules, and one draw needn't show every extreme that they name: `queries`: entries stay within -6 to 6. `passage_keys`: entries stay within -6 to 6. `retrieved`: passage m belongs to owner m // 16. The 2 rows of one device (aligned blocks of 2 rows) hold only different ids, and at most 2 of them belong to one owner; in every block some owner has exactly 2.
All inputs are finite; a program needn't handle non-finite values.
Results may differ from the reference program's by a relative error of at most 0.0085.
Values may be sent and summed in bfloat16 or wider, within the bound.
No kernel may reach another device: no remote copies, remote signals or barrier semaphores. Data moves between devices by JAX's collectives and lax.ppermute only.
A program may use at most 64 MiB of HBM per device.

```python
import math
import jax
import jax.numpy as jnp
from jax import lax

HQ = 32
KVH = 4
HD = 128
QLEN = 64
Q_DEV = 2
K_RET = 32
PLEN = 4
P_DEV = 16
CAP = 2
QUERIES = 1024
PASSAGES = 1024
N_PAS = 64


def draw_queries(key, part):
    key = jax.random.fold_in(key, 11)
    shape = (QUERIES * QLEN, HQ * HD)
    values = jnp.clip(jax.random.normal(key, shape, jnp.float32), -6.0, 6.0)
    return values.astype(jnp.bfloat16)


def draw_passage_keys(key, part):
    key = jax.random.fold_in(key, 23)
    shape = (PASSAGES, PLEN, KVH * HD)
    values = jnp.clip(jax.random.normal(key, shape, jnp.float32), -6.0, 6.0)
    return values.astype(jnp.bfloat16)


def device_requests(device_key):
    slot_total = N_PAS * CAP
    request_total = Q_DEV * K_RET
    perm_key, first_key, second_key = jax.random.split(device_key, 3)
    shuffled = jax.random.permutation(perm_key, slot_total)
    ranking = jnp.argsort(shuffled, stable=True).astype(jnp.int32)
    positions = jnp.arange(slot_total, dtype=jnp.int32)
    owner_at = positions % N_PAS
    repeat_at = positions // N_PAS
    forced = shuffled[0] % N_PAS
    priority = jnp.where(owner_at == forced, repeat_at - CAP, ranking)
    chosen = jnp.argsort(priority, stable=True)[:request_total].astype(jnp.int32)
    owners = chosen % N_PAS
    repeats = chosen // N_PAS
    offsets = jnp.minimum(jax.random.randint(first_key, (N_PAS,), 0, P_DEV), jax.random.randint(second_key, (N_PAS,), 0, P_DEV))
    local_ids = (offsets[owners] + repeats) % P_DEV
    return (owners * P_DEV + local_ids).astype(jnp.int32).reshape(Q_DEV, K_RET)


def draw_retrieved(key, part):
    key = jax.random.fold_in(key, 37)
    device_keys = jax.random.split(key, QUERIES // Q_DEV)
    blocks = jax.vmap(device_requests)(device_keys)
    return blocks.reshape(QUERIES, K_RET)


def with_ends(values, key, smallest, top_value):
    index_at = [jax.random.randint(jax.random.fold_in(key, axis), (), 0, length) for axis, length in enumerate(values.shape)]
    main_axis = values.shape.index(max(values.shape))
    beside = index_at[:main_axis] + [(index_at[main_axis] + 1) % values.shape[main_axis]] + index_at[main_axis + 1:]
    return values.at[tuple(index_at)].set(smallest).at[tuple(beside)].set(top_value)


def levels(own_key, dims, cuts, least, largest):
    loudness = 1.0
    for dim, shards_of in cuts:
        heights = jax.random.uniform(jax.random.fold_in(jax.random.fold_in(own_key, 6), dim), (shards_of,), jnp.float32, least / len(cuts), largest / len(cuts))
        loudness = loudness * jnp.repeat(jnp.exp(heights), dims[dim] // shards_of).reshape((-1,) + (1,) * (len(dims) - 1 - dim))
    return loudness


def noise(stream_key, extent, spread, most, cuts=(), held_as=jnp.bfloat16):
    values = spread * jax.random.normal(stream_key, extent, jnp.float32)
    if cuts:
        values = values * levels(stream_key, extent, cuts, -0.22, 0.18)
    return jnp.clip(values, -most, most).astype(held_as)


def setup_inputs(seed: int = 0) -> dict:
    seeds = jax.random.split(jax.random.key(seed), 9)
    queries = draw_queries(jax.random.fold_in(seeds[8], 71), 0)
    grad_out = noise(seeds[1], (QUERIES * QLEN, HQ * HD), 1.0, 6.0, ((0, 512),))
    suffix_keys = noise(seeds[2], (QUERIES * QLEN, KVH * HD), 1.0, 6.0, ((0, 512),))
    suffix_values = noise(seeds[3], (QUERIES * QLEN, KVH * HD), 1.0, 6.0, ((0, 512),))
    passage_keys = draw_passage_keys(jax.random.fold_in(seeds[8], 71), 0)
    passage_values = noise(seeds[5], (PASSAGES, PLEN, KVH * HD), 1.0, 6.0, ((0, 64),))
    passage_lengths = with_ends(jax.random.randint(seeds[6], (PASSAGES,), 1, PLEN + 1), jax.random.fold_in(seeds[6], 1), 1, PLEN).astype(jnp.int32)
    retrieved = draw_retrieved(jax.random.fold_in(seeds[8], 71), 0)
    return dict(queries=queries, grad_out=grad_out, suffix_keys=suffix_keys, suffix_values=suffix_values, passage_keys=passage_keys, passage_values=passage_values, passage_lengths=passage_lengths, retrieved=retrieved)


def attend(query_block, grad_block, key_rows, value_rows, allowed):
    score_scale = 1.0 / math.sqrt(HD)
    query_wide = query_block.astype(jnp.float32)
    grad_wide = grad_block.astype(jnp.float32)
    key_wide = key_rows.astype(jnp.float32)
    value_wide = value_rows.astype(jnp.float32)
    scores = jnp.einsum('igxd,jgd->gxij', query_wide, key_wide) * score_scale
    scores = jnp.where(allowed[None, None], scores, -jnp.inf)
    row_top = lax.optimization_barrier(jnp.max(scores, axis=-1, keepdims=True))
    raised = jnp.exp(scores - row_top)
    probabilities = raised / lax.optimization_barrier(jnp.sum(raised, axis=-1, keepdims=True))
    weights = lax.optimization_barrier(probabilities.astype(jnp.bfloat16)).astype(jnp.float32)
    attended = jnp.einsum('gxij,jgd->igxd', weights, value_wide)
    row_delta = lax.optimization_barrier(jnp.sum(grad_wide * attended, axis=-1))
    prob_grad = jnp.einsum('igxd,jgd->gxij', grad_wide, value_wide)
    dscore = probabilities * (prob_grad - jnp.transpose(row_delta, (1, 2, 0))[..., None])
    dscore_half = lax.optimization_barrier(dscore.astype(jnp.bfloat16)).astype(jnp.float32)
    grad_query = jnp.einsum('gxij,jgd->igxd', dscore_half, key_wide) * score_scale
    grad_key = jnp.einsum('gxij,igxd->jgd', dscore_half, query_wide) * score_scale
    grad_value = jnp.einsum('gxij,igxd->jgd', weights, grad_wide)
    return (grad_query, grad_key, grad_value)

def reference(queries, grad_out, suffix_keys, suffix_values, passage_keys, passage_values, passage_lengths, retrieved):
    group_size = HQ // KVH
    pair_width = KVH * HD
    passage_rows = K_RET * PLEN
    positions = jnp.arange(PLEN, dtype=jnp.int32)
    suffix_positions = jnp.arange(QLEN, dtype=jnp.int32)
    causal = suffix_positions[None, :] <= suffix_positions[:, None]

    def per_query(running, query_index):
        key_total, value_total = running
        passage_ids = retrieved[query_index]
        row_start = (query_index * QLEN).astype(jnp.int32)
        query_block = lax.dynamic_slice_in_dim(queries, row_start, QLEN, 0).reshape(QLEN, KVH, group_size, HD)
        grad_block = lax.dynamic_slice_in_dim(grad_out, row_start, QLEN, 0).reshape(QLEN, KVH, group_size, HD)
        own_keys = lax.dynamic_slice_in_dim(suffix_keys, row_start, QLEN, 0).reshape(QLEN, KVH, HD)
        own_values = lax.dynamic_slice_in_dim(suffix_values, row_start, QLEN, 0).reshape(QLEN, KVH, HD)
        key_rows = jnp.concatenate([passage_keys[passage_ids].reshape(passage_rows, KVH, HD), own_keys], axis=0)
        value_rows = jnp.concatenate([passage_values[passage_ids].reshape(passage_rows, KVH, HD), own_values], axis=0)
        live_keys = (positions[None, :] < passage_lengths[passage_ids][:, None]).reshape(-1)
        allowed = jnp.concatenate([jnp.broadcast_to(live_keys[None, :], (QLEN, passage_rows)), causal], axis=1)
        grad_query, grad_key, grad_value = attend(query_block, grad_block, key_rows, value_rows, allowed)
        key_term = lax.optimization_barrier(grad_key[:passage_rows].astype(jnp.bfloat16)).astype(jnp.float32)
        value_term = lax.optimization_barrier(grad_value[:passage_rows].astype(jnp.bfloat16)).astype(jnp.float32)
        key_total = key_total.at[passage_ids].add(key_term.reshape(K_RET, PLEN, pair_width))
        value_total = value_total.at[passage_ids].add(value_term.reshape(K_RET, PLEN, pair_width))
        outputs = (grad_query.reshape(QLEN, HQ * HD).astype(jnp.bfloat16), grad_key[passage_rows:].reshape(QLEN, pair_width).astype(jnp.bfloat16), grad_value[passage_rows:].reshape(QLEN, pair_width).astype(jnp.bfloat16))
        return ((key_total, value_total), outputs)
    initial = (jnp.zeros((PASSAGES, PLEN, pair_width), jnp.float32), jnp.zeros((PASSAGES, PLEN, pair_width), jnp.float32))
    totals, stacked = lax.scan(per_query, initial, jnp.arange(QUERIES, dtype=jnp.int32))
    grad_queries = stacked[0].reshape(QUERIES * QLEN, HQ * HD)
    grad_suffix_keys = stacked[1].reshape(QUERIES * QLEN, pair_width)
    grad_suffix_values = stacked[2].reshape(QUERIES * QLEN, pair_width)
    return (grad_queries, grad_suffix_keys, grad_suffix_values, totals[0].astype(jnp.bfloat16), totals[1].astype(jnp.bfloat16))
```

```python
import functools
import math

import jax
import jax.numpy as jnp
from jax import lax
from jax.experimental import pallas as pl
from jax.experimental.pallas import tpu as pltpu
from jax.sharding import PartitionSpec as P

HQ = 32
HD = 128
CAP = 2
DEAD = 16.0
NEG = -1e30
BF = jnp.bfloat16
F32 = jnp.float32


def iota(shape, dim):
    return lax.broadcasted_iota(jnp.int32, shape, dim)


def dot(a, b, ca=1, cb=0):
    return lax.dot_general(a, b, (((ca,), (cb,)), ((), ())), preferred_element_type=F32)


def one(mask, dtype=BF):
    return jnp.where(mask, 1.0, 0.0).astype(dtype)


def slot_masks(ids, owners, n_local, plen):
    n_query, n_ret = ids.shape
    lanes = n_ret * plen
    own = lax.div(ids, n_local)
    loc = ids - own * n_local
    spread = one(iota((n_ret, lanes), 1) // plen == iota((n_ret, lanes), 0), F32)
    own = dot(own.astype(F32), spread).astype(jnp.int32)
    loc = dot(loc.astype(F32), spread)
    before = one(
        (iota((lanes, lanes), 0) % plen == 0)
        & (iota((lanes, lanes), 0) // plen < iota((lanes, lanes), 1) // plen)
    )
    heads = one(iota((lanes, lanes), 0) % plen == 0)
    masks = []
    locals_ = []
    used = None
    for n in range(n_query):
        hit = iota((owners, lanes), 0) == own[n : n + 1]
        hit_b = one(hit)
        rank = dot(hit_b, before)
        if used is not None:
            rank = rank + used
        total = dot(hit_b, heads)
        used = total if used is None else used + total
        masks.append([one(hit & (rank == float(c)), F32) for c in range(CAP)])
        locals_.append(loc[n : n + 1])
    return masks, locals_


def request_kernel(owners, n_local, plen, ids_ref, req_ref):
    masks, locs = slot_masks(ids_ref[...], owners, n_local, plen)
    lanes = locs[0].shape[1]
    first = iota((owners, lanes), 1) % plen == 0
    wanted = []
    for c in range(CAP):
        total = 0.0
        for mask, loc in zip(masks, locs):
            total = total + mask[c] * (loc + 1.0)
        wanted.append(jnp.sum(jnp.where(first, total, 0.0), axis=1, keepdims=True))
    width = CAP * n_local * plen
    lane = iota((owners, width), 1)
    slot = lane // (n_local * plen)
    local = (lane % (n_local * plen)) // plen
    picked = jnp.where(slot == 0, wanted[0], wanted[1])
    req_ref[...] = one(picked == (local + 1).astype(F32), F32)


def owner_kernel(owners, n_local, plen, req_ref, len_ref, pk_ref, pv_ref, send_ref, table_ref):
    rows = owners * CAP * plen
    width = CAP * n_local * plen
    chunk = CAP * plen
    who = one(iota((rows, owners), 0) // chunk == iota((rows, owners), 1))
    spread = dot(who, req_ref[...].astype(BF))
    row = iota((rows, width), 0)
    lane = iota((rows, width), 1)
    same = ((row % chunk) // plen == lane // (n_local * plen)) & (row % plen == lane % plen)
    lane_row = iota((1, width), 1)
    lane_m = (lane_row % (n_local * plen)) // plen
    live = jnp.zeros((1, width), jnp.int32)
    for m in range(n_local):
        live = jnp.where(lane_m == m, len_ref[m], live)
    live = lane_row % plen < live
    table = jnp.where(same & live, spread, 0.0).astype(BF)
    table_ref[...] = table
    alive = dot(table, jnp.ones((width, HD), BF))
    fill = (1.0 - alive) * DEAD
    keys = jnp.concatenate([pk_ref[...]] * CAP, axis=0)
    values = jnp.concatenate([pv_ref[...]] * CAP, axis=0)
    kv_width = keys.shape[1]
    sent_keys = dot(table, keys)
    fill = jnp.concatenate([fill] * (kv_width // HD), axis=1)
    send_ref[:, :kv_width] = (sent_keys + fill).astype(BF)
    send_ref[:, kv_width:] = dot(table, values).astype(BF)


def attend_kernel(
    owners,
    n_local,
    plen,
    ids_ref,
    recv_ref,
    q_ref,
    g_ref,
    sk_ref,
    sv_ref,
    dq_ref,
    dsk_ref,
    dsv_ref,
    terms_ref,
    place_ref,
    kv_ref,
    out_ref,
):
    n_query, n_ret = ids_ref.shape
    lanes = n_ret * plen
    rows = owners * CAP * plen
    chunk = CAP * plen
    kv_width = sk_ref.shape[1]
    kv_heads = kv_width // HD
    group = HQ // kv_heads
    q_len = q_ref.shape[0] // n_query
    scale = 1.0 / math.sqrt(HD)
    log2e = 1.4426950408889634

    masks, _ = slot_masks(ids_ref[...], owners, n_local, plen)
    row = iota((rows, CAP * owners), 0)
    lane = iota((rows, CAP * owners), 1)
    who = one((row // chunk == lane % owners) & ((row % chunk) // plen == lane // owners))
    same = iota((rows, lanes), 0) % plen == iota((rows, lanes), 1) % plen
    for n in range(n_query):
        asked = jnp.concatenate([m.astype(BF) for m in masks[n]], axis=0)
        place_ref[:, n * lanes : (n + 1) * lanes] = jnp.where(same, dot(who, asked), 0.0).astype(BF)
    kv_ref[...] = dot(place_ref[...], recv_ref[...], 0, 0).astype(BF)

    causal = iota((q_len, group * q_len), 0) <= iota((q_len, group * q_len), 1) % q_len
    for g in range(kv_heads):
        col = g * HD
        vcol = kv_width + g * HD
        for n in range(n_query):
            r0 = n * q_len
            k0 = n * lanes
            q = jnp.concatenate(
                [
                    q_ref[r0 : r0 + q_len, (g * group + x) * HD : (g * group + x + 1) * HD]
                    for x in range(group)
                ],
                axis=0,
            )
            go = jnp.concatenate(
                [
                    g_ref[r0 : r0 + q_len, (g * group + x) * HD : (g * group + x + 1) * HD]
                    for x in range(group)
                ],
                axis=0,
            )
            pk = kv_ref[k0 : k0 + lanes, col : col + HD]
            keys = jnp.concatenate([pk, sk_ref[r0 : r0 + q_len, col : col + HD]], axis=0)
            values = jnp.concatenate(
                [kv_ref[k0 : k0 + lanes, vcol : vcol + HD], sv_ref[r0 : r0 + q_len, col : col + HD]],
                axis=0,
            )
            s = dot(keys, q, 1, 1) * (scale * log2e)
            alive = pk.astype(F32) < 0.5 * DEAD
            alive = jnp.concatenate([alive] * (group * q_len // HD), axis=1)
            s = jnp.concatenate(
                [jnp.where(alive, s[:lanes], NEG), jnp.where(causal, s[lanes:], NEG)], axis=0
            )
            e = jnp.exp2(s - jnp.max(s, axis=0, keepdims=True))
            p = e * (1.0 / jnp.sum(e, axis=0, keepdims=True))
            w = p.astype(BF)
            dp = dot(values, go, 1, 1)
            delta = jnp.sum(w.astype(F32) * dp, axis=0, keepdims=True)
            ds = (p * (dp - delta)).astype(BF)
            dv = dot(w, go)
            dk = dot(ds, q) * scale
            dq = (dot(ds, keys, 0, 0) * scale).astype(BF)
            for x in range(group):
                dq_ref[r0 : r0 + q_len, (g * group + x) * HD : (g * group + x + 1) * HD] = dq[
                    x * q_len : (x + 1) * q_len
                ]
            dsk_ref[r0 : r0 + q_len, col : col + HD] = dk[lanes:].astype(BF)
            dsv_ref[r0 : r0 + q_len, col : col + HD] = dv[lanes:].astype(BF)
            out_ref[k0 : k0 + lanes, col : col + HD] = dk[:lanes].astype(BF)
            out_ref[k0 : k0 + lanes, vcol : vcol + HD] = dv[:lanes].astype(BF)
    terms_ref[...] = dot(place_ref[...], out_ref[...]).astype(BF)


def owner_sum_kernel(table_ref, back_ref, sum_ref):
    total = dot(table_ref[...], back_ref[...], 0, 0)
    half = total.shape[0] // CAP
    sum_ref[...] = (total[:half] + total[half:]).astype(BF)


def final_kernel(parts_ref, gk_ref, gv_ref):
    total = jnp.sum(parts_ref[...].astype(F32), axis=0).astype(BF)
    n_out, plen, kv_width = gk_ref.shape
    for m in range(n_out):
        gk_ref[m] = total[m * plen : (m + 1) * plen, :kv_width]
        gv_ref[m] = total[m * plen : (m + 1) * plen, kv_width:]


VMEM = pl.BlockSpec(memory_space=pltpu.VMEM)
SMEM = pl.BlockSpec(memory_space=pltpu.SMEM)


def call(kernel, out_shape, in_specs, n_out, name, limit=16, scratch=()):
    return pl.pallas_call(
        kernel,
        out_shape=out_shape,
        in_specs=in_specs,
        out_specs=[VMEM] * n_out if n_out > 1 else VMEM,
        scratch_shapes=list(scratch),
        compiler_params=pltpu.CompilerParams(vmem_limit_bytes=limit * 2**20),
        name=name,
    )


def on_device(
    queries,
    grad_out,
    suffix_keys,
    suffix_values,
    passage_keys,
    passage_values,
    passage_lengths,
    retrieved,
):
    owners = lax.axis_size("pas")
    groups = lax.axis_size("qry")
    n_local, plen, kv_width = passage_keys.shape
    n_query, n_ret = retrieved.shape
    lanes = n_ret * plen
    rows = owners * CAP * plen
    width = CAP * n_local * plen
    sds = jax.ShapeDtypeStruct
    dims = (owners, n_local, plen)

    request = call(
        functools.partial(request_kernel, *dims), sds((owners, width), F32), [VMEM], 1, "request"
    )(retrieved)
    asked = lax.all_to_all(
        request.reshape(owners, 1, width), "pas", split_axis=0, concat_axis=0, tiled=True
    ).reshape(owners, width)

    flat_keys = passage_keys.reshape(n_local * plen, kv_width)
    flat_values = passage_values.reshape(n_local * plen, kv_width)
    send, table = call(
        functools.partial(owner_kernel, *dims),
        [sds((rows, 2 * kv_width), BF), sds((rows, width), BF)],
        [VMEM, SMEM, VMEM, VMEM],
        2,
        "owner_gather",
    )(asked, passage_lengths, flat_keys, flat_values)
    recv = lax.all_to_all(
        send.reshape(owners, CAP * plen, 2 * kv_width), "pas", split_axis=0, concat_axis=0, tiled=True
    ).reshape(rows, 2 * kv_width)

    dq, dsk, dsv, terms = call(
        functools.partial(attend_kernel, *dims),
        [
            sds(queries.shape, BF),
            sds(suffix_keys.shape, BF),
            sds(suffix_values.shape, BF),
            sds((rows, 2 * kv_width), BF),
        ],
        [VMEM] * 6,
        4,
        "attend",
        limit=32,
        scratch=[
            pltpu.VMEM((rows, n_query * lanes), BF),
            pltpu.VMEM((n_query * lanes, 2 * kv_width), BF),
            pltpu.VMEM((n_query * lanes, 2 * kv_width), BF),
        ],
    )(retrieved, recv, queries, grad_out, suffix_keys, suffix_values)
    back = lax.all_to_all(
        terms.reshape(owners, CAP * plen, 2 * kv_width), "pas", split_axis=0, concat_axis=0, tiled=True
    ).reshape(rows, 2 * kv_width)

    sums = call(owner_sum_kernel, sds((n_local * plen, 2 * kv_width), BF), [VMEM] * 2, 1, "owner_sum")(
        table, back
    )
    parts = lax.all_to_all(
        sums.reshape(groups, n_local // groups * plen, 2 * kv_width),
        "qry",
        split_axis=0,
        concat_axis=0,
        tiled=True,
    )
    out = sds((n_local // groups, plen, kv_width), BF)
    gk, gv = call(final_kernel, [out, out], [VMEM], 2, "final_sum")(parts)
    return dq, dsk, dsv, gk, gv


def solution(mesh):
    in_specs = (
        P(("pas", "qry"), None),
        P(("pas", "qry"), None),
        P(("pas", "qry"), None),
        P(("pas", "qry"), None),
        P("pas", None, None),
        P("pas", None, None),
        P("pas"),
        P(("pas", "qry"), None),
    )
    out_specs = (
        P(("pas", "qry"), None),
        P(("pas", "qry"), None),
        P(("pas", "qry"), None),
        P(("pas", "qry"), None, None),
        P(("pas", "qry"), None, None),
    )
    return jax.shard_map(
        on_device, mesh=mesh, in_specs=in_specs, out_specs=out_specs, check_vma=False
    )
```

```python
import functools
import math

import jax
import jax.numpy as jnp
from jax import lax
from jax.experimental import pallas as pl
from jax.experimental.pallas import tpu as pltpu
from jax.sharding import PartitionSpec as P

HQ = 32
HD = 128
CAP = 2
DEAD = 16.0
NEG = -1e30
SCALE = 1.0 / math.sqrt(HD)
SCALE2 = SCALE * math.log2(math.e)
BF = jnp.bfloat16
F32 = jnp.float32


def iota(shape, dim):
    return lax.broadcasted_iota(jnp.int32, shape, dim)


def dot(a, b, ca=1, cb=0):
    return lax.dot_general(a, b, (((ca,), (cb,)), ((), ())), preferred_element_type=F32)


def one(mask, dtype=BF):
    return jnp.where(mask, 1.0, 0.0).astype(dtype)


def slot_masks(ids, owners, n_local, plen):
    n_query, n_ret = ids.shape
    lanes = n_ret * plen
    own = lax.div(ids, n_local)
    loc = ids - own * n_local
    spread = one(iota((n_ret, lanes), 1) // plen == iota((n_ret, lanes), 0), F32)
    own = dot(own.astype(F32), spread).astype(jnp.int32)
    loc = dot(loc.astype(F32), spread)
    before = one(
        (iota((lanes, lanes), 0) % plen == 0)
        & (iota((lanes, lanes), 0) // plen < iota((lanes, lanes), 1) // plen)
    )
    heads = one(iota((lanes, lanes), 0) % plen == 0)
    masks = []
    locals_ = []
    used = None
    for n in range(n_query):
        hit = iota((owners, lanes), 0) == own[n : n + 1]
        hit_b = one(hit)
        rank = dot(hit_b, before)
        if used is not None:
            rank = rank + used
        total = dot(hit_b, heads)
        used = total if used is None else used + total
        masks.append([one(hit & (rank == float(c)), F32) for c in range(CAP)])
        locals_.append(loc[n : n + 1])
    return masks, locals_


def request_kernel(owners, n_local, plen, ids_ref, req_ref):
    masks, locs = slot_masks(ids_ref[...], owners, n_local, plen)
    lanes = locs[0].shape[1]
    first = iota((owners, lanes), 1) % plen == 0
    wanted = []
    for c in range(CAP):
        total = 0.0
        for mask, loc in zip(masks, locs):
            total = total + mask[c] * (loc + 1.0)
        wanted.append(jnp.sum(jnp.where(first, total, 0.0), axis=1, keepdims=True))
    width = CAP * n_local * plen
    lane = iota((owners, width), 1)
    slot = lane // (n_local * plen)
    local = (lane % (n_local * plen)) // plen
    picked = jnp.where(slot == 0, wanted[0], wanted[1])
    req_ref[...] = one(picked == (local + 1).astype(F32), F32)


def owner_prepare_kernel(owners, n_local, plen, len_ref, pk_ref, pv_ref, mask_ref, kv_ref):
    rows = owners * CAP * plen
    width = CAP * n_local * plen
    chunk = CAP * plen
    row = iota((rows, width), 0)
    lane = iota((rows, width), 1)
    same = ((row % chunk) // plen == lane // (n_local * plen)) & (row % plen == lane % plen)
    lane_row = iota((1, width), 1)
    lane_m = (lane_row % (n_local * plen)) // plen
    live = jnp.zeros((1, width), jnp.int32)
    for m in range(n_local):
        live = jnp.where(lane_m == m, len_ref[m], live)
    live = lane_row % plen < live
    mask_ref[...] = one(same & live, F32)
    kv_width = pk_ref.shape[1]
    half = n_local * plen
    for c in range(CAP):
        kv_ref[c * half : (c + 1) * half, :kv_width] = pk_ref[...]
        kv_ref[c * half : (c + 1) * half, kv_width:] = pv_ref[...]


def owner_kernel(owners, plen, req_ref, mask_ref, kv_ref, send_ref, table_ref):
    rows, width = mask_ref.shape
    chunk = CAP * plen
    who = one(iota((rows, owners), 0) // chunk == iota((rows, owners), 1))
    spread = dot(who, req_ref[...].astype(BF))
    table = (spread * mask_ref[...]).astype(BF)
    table_ref[...] = table
    alive = dot(table, jnp.ones((width, HD), BF))
    fill = (1.0 - alive) * DEAD
    kv_width = kv_ref.shape[1] // 2
    sent = dot(table, kv_ref[...])
    for g in range(kv_width // HD):
        send_ref[:, g * HD : (g + 1) * HD] = (sent[:, g * HD : (g + 1) * HD] + fill).astype(BF)
    send_ref[:, kv_width:] = sent[:, kv_width:].astype(BF)


def attend_prepare_kernel(
    owners,
    n_local,
    plen,
    ids_ref,
    q_ref,
    g_ref,
    sk_ref,
    sv_ref,
    place_ref,
    qh_ref,
    gh_ref,
    s_ref,
    dp_ref,
):
    n_query, n_ret = ids_ref.shape
    lanes = n_ret * plen
    rows = owners * CAP * plen
    chunk = CAP * plen
    kv_heads = sk_ref.shape[1] // HD
    group = HQ // kv_heads
    q_len = q_ref.shape[0] // n_query

    masks, _ = slot_masks(ids_ref[...], owners, n_local, plen)
    row = iota((rows, CAP * owners), 0)
    lane = iota((rows, CAP * owners), 1)
    who = one((row // chunk == lane % owners) & ((row % chunk) // plen == lane // owners))
    same = iota((rows, lanes), 0) % plen == iota((rows, lanes), 1) % plen
    for n in range(n_query):
        asked = jnp.concatenate([m.astype(BF) for m in masks[n]], axis=0)
        place_ref[:, n * lanes : (n + 1) * lanes] = jnp.where(same, dot(who, asked), 0.0).astype(BF)

    causal = iota((q_len, group * q_len), 0) <= iota((q_len, group * q_len), 1) % q_len
    for n in range(n_query):
        r0 = n * q_len
        for g in range(kv_heads):
            at = n * kv_heads + g
            for x in range(group):
                col = (g * group + x) * HD
                qh_ref[at, x * q_len : (x + 1) * q_len] = q_ref[r0 : r0 + q_len, col : col + HD]
                gh_ref[at, x * q_len : (x + 1) * q_len] = g_ref[r0 : r0 + q_len, col : col + HD]
            keys = sk_ref[r0 : r0 + q_len, g * HD : (g + 1) * HD]
            values = sv_ref[r0 : r0 + q_len, g * HD : (g + 1) * HD]
            s = dot(keys, qh_ref[at], 1, 1) * SCALE2
            s_ref[at] = jnp.where(causal, s, NEG)
            dp_ref[at] = dot(values, gh_ref[at], 1, 1)


def attend_kernel(
    place_ref,
    recv_ref,
    qh_ref,
    gh_ref,
    s_ref,
    dp_ref,
    terms_ref,
    kv_ref,
    ds_ref,
    w_ref,
    out_ref,
):
    pairs, wide, _ = qh_ref.shape
    kv_width = recv_ref.shape[1] // 2
    kv_heads = kv_width // HD
    n_query = pairs // kv_heads
    lanes = place_ref.shape[1] // n_query
    kv_ref[...] = dot(place_ref[...], recv_ref[...], 0, 0).astype(BF)
    for n in range(n_query):
        k0 = n * lanes
        for g in range(kv_heads):
            at = n * kv_heads + g
            col = g * HD
            vcol = kv_width + g * HD
            q = qh_ref[at]
            go = gh_ref[at]
            pk = kv_ref[k0 : k0 + lanes, col : col + HD]
            pv = kv_ref[k0 : k0 + lanes, vcol : vcol + HD]
            alive = pk.astype(F32) < 0.5 * DEAD
            alive = jnp.concatenate([alive] * (wide // HD), axis=1)
            s_p = jnp.where(alive, dot(pk, q, 1, 1) * SCALE2, NEG)
            s_s = s_ref[at]
            top = jnp.maximum(
                jnp.max(s_p, axis=0, keepdims=True), jnp.max(s_s, axis=0, keepdims=True)
            )
            e_p = jnp.exp2(s_p - top)
            e_s = jnp.exp2(s_s - top)
            share = 1.0 / (
                jnp.sum(e_p, axis=0, keepdims=True) + jnp.sum(e_s, axis=0, keepdims=True)
            )
            p_p = e_p * share
            p_s = e_s * share
            w_p = p_p.astype(BF)
            w_s = p_s.astype(BF)
            dp_p = dot(pv, go, 1, 1)
            dp_s = dp_ref[at]
            delta = jnp.sum(w_p.astype(F32) * dp_p, axis=0, keepdims=True) + jnp.sum(
                w_s.astype(F32) * dp_s, axis=0, keepdims=True
            )
            ds_p = (p_p * (dp_p - delta)).astype(BF)
            ds_s = (p_s * (dp_s - delta)).astype(BF)
            out_ref[k0 : k0 + lanes, col : col + HD] = (dot(ds_p, q) * SCALE).astype(BF)
            out_ref[k0 : k0 + lanes, vcol : vcol + HD] = dot(w_p, go).astype(BF)
            ds_ref[at, :lanes] = ds_p
            ds_ref[at, lanes:] = ds_s
            w_ref[at] = w_s
    terms_ref[...] = dot(place_ref[...], out_ref[...]).astype(BF)


def attend_rest_kernel(kv_ref, ds_ref, w_ref, qh_ref, gh_ref, sk_ref, dq_ref, dsk_ref, dsv_ref):
    pairs, wide, _ = qh_ref.shape
    kv_heads = sk_ref.shape[1] // HD
    n_query = pairs // kv_heads
    lanes = kv_ref.shape[0] // n_query
    q_len = sk_ref.shape[0] // n_query
    group = wide // q_len
    for n in range(n_query):
        r0 = n * q_len
        for g in range(kv_heads):
            at = n * kv_heads + g
            col = g * HD
            ds = ds_ref[at]
            keys = jnp.concatenate(
                [
                    kv_ref[n * lanes : (n + 1) * lanes, col : col + HD],
                    sk_ref[r0 : r0 + q_len, col : col + HD],
                ],
                axis=0,
            )
            dq = (dot(ds, keys, 0, 0) * SCALE).astype(BF)
            for x in range(group):
                at_col = (g * group + x) * HD
                dq_ref[r0 : r0 + q_len, at_col : at_col + HD] = dq[x * q_len : (x + 1) * q_len]
            dsk = dot(ds[lanes:], qh_ref[at]) * SCALE
            dsk_ref[r0 : r0 + q_len, col : col + HD] = dsk.astype(BF)
            dsv_ref[r0 : r0 + q_len, col : col + HD] = dot(w_ref[at], gh_ref[at]).astype(BF)


def owner_sum_kernel(table_ref, back_ref, sum_ref):
    total = dot(table_ref[...], back_ref[...], 0, 0)
    half = total.shape[0] // CAP
    sum_ref[...] = (total[:half] + total[half:]).astype(BF)


def final_kernel(parts_ref, gk_ref, gv_ref):
    total = jnp.sum(parts_ref[...].astype(F32), axis=0).astype(BF)
    n_out, plen, kv_width = gk_ref.shape
    for m in range(n_out):
        gk_ref[m] = total[m * plen : (m + 1) * plen, :kv_width]
        gv_ref[m] = total[m * plen : (m + 1) * plen, kv_width:]


VMEM = pl.BlockSpec(memory_space=pltpu.VMEM)
SMEM = pl.BlockSpec(memory_space=pltpu.SMEM)


def call(kernel, out_shape, in_specs, name, limit=16, scratch=(), cost=None):
    several = isinstance(out_shape, (list, tuple))
    return pl.pallas_call(
        kernel,
        out_shape=out_shape,
        in_specs=in_specs,
        out_specs=[VMEM] * len(out_shape) if several else VMEM,
        scratch_shapes=list(scratch),
        compiler_params=pltpu.CompilerParams(vmem_limit_bytes=limit * 2**20),
        cost_estimate=cost,
        name=name,
    )


def cost(flops, mib, exps=0):
    return pl.CostEstimate(
        flops=int(flops), bytes_accessed=int(mib * 2**20), transcendentals=int(exps)
    )


def on_device(
    queries,
    grad_out,
    suffix_keys,
    suffix_values,
    passage_keys,
    passage_values,
    passage_lengths,
    retrieved,
):
    owners = lax.axis_size("pas")
    groups = lax.axis_size("qry")
    n_local, plen, kv_width = passage_keys.shape
    n_query, n_ret = retrieved.shape
    lanes = n_ret * plen
    rows = owners * CAP * plen
    width = CAP * n_local * plen
    kv_heads = kv_width // HD
    pairs = n_query * kv_heads
    q_len = queries.shape[0] // n_query
    wide = HQ // kv_heads * q_len
    sds = jax.ShapeDtypeStruct
    dims = (owners, n_local, plen)

    def exchange(x):
        parts = x.reshape((owners, rows // owners, x.shape[1]))
        return lax.all_to_all(parts, "pas", split_axis=0, concat_axis=0, tiled=True).reshape(x.shape)

    request = call(
        functools.partial(request_kernel, *dims), sds((owners, width), F32), [VMEM], "request"
    )(retrieved)
    asked = lax.all_to_all(
        request.reshape(owners, 1, width), "pas", split_axis=0, concat_axis=0, tiled=True
    ).reshape(owners, width)

    mask, tables = call(
        functools.partial(owner_prepare_kernel, *dims),
        [sds((rows, width), F32), sds((width, 2 * kv_width), BF)],
        [SMEM, VMEM, VMEM],
        "owner_prepare",
        cost=cost(1e6, 1),
    )(
        passage_lengths,
        passage_keys.reshape(n_local * plen, kv_width),
        passage_values.reshape(n_local * plen, kv_width),
    )
    send, table = call(
        functools.partial(owner_kernel, owners, plen),
        [sds((rows, 2 * kv_width), BF), sds((rows, width), BF)],
        [VMEM, VMEM, VMEM],
        "owner_gather",
    )(asked, mask, tables)
    recv = exchange(send)

    place, qh, gh, s_suf, dp_suf = call(
        functools.partial(attend_prepare_kernel, *dims),
        [
            sds((rows, n_query * lanes), BF),
            sds((pairs, wide, HD), BF),
            sds((pairs, wide, HD), BF),
            sds((pairs, q_len, wide), F32),
            sds((pairs, q_len, wide), F32),
        ],
        [VMEM] * 5,
        "attend_prepare",
        cost=cost(4 * pairs * wide * q_len * HD, 7),
    )(retrieved, queries, grad_out, suffix_keys, suffix_values)
    terms, kv, ds, w_suf = call(
        attend_kernel,
        [
            sds((rows, 2 * kv_width), BF),
            sds((n_query * lanes, 2 * kv_width), BF),
            sds((pairs, lanes + q_len, wide), BF),
            sds((pairs, q_len, wide), BF),
        ],
        [VMEM] * 6,
        "attend",
        scratch=[pltpu.VMEM((n_query * lanes, 2 * kv_width), BF)],
    )(place, recv, qh, gh, s_suf, dp_suf)
    back = exchange(terms)

    dq, dsk, dsv = call(
        attend_rest_kernel,
        [sds(queries.shape, BF), sds(suffix_keys.shape, BF), sds(suffix_values.shape, BF)],
        [VMEM] * 6,
        "attend_rest",
        cost=cost(8 * pairs * wide * (lanes + q_len) * HD, 6),
    )(kv, ds, w_suf, qh, gh, suffix_keys)

    sums = call(owner_sum_kernel, sds((n_local * plen, 2 * kv_width), BF), [VMEM] * 2, "owner_sum")(
        table, back
    )
    parts = lax.all_to_all(
        sums.reshape(groups, n_local // groups * plen, 2 * kv_width),
        "qry",
        split_axis=0,
        concat_axis=0,
        tiled=True,
    )
    out = sds((n_local // groups, plen, kv_width), BF)
    gk, gv = call(final_kernel, [out, out], [VMEM], "final_sum")(parts)
    return dq, dsk, dsv, gk, gv


def solution(mesh):
    in_specs = (
        P(("pas", "qry"), None),
        P(("pas", "qry"), None),
        P(("pas", "qry"), None),
        P(("pas", "qry"), None),
        P("pas", None, None),
        P("pas", None, None),
        P("pas"),
        P(("pas", "qry"), None),
    )
    out_specs = (
        P(("pas", "qry"), None),
        P(("pas", "qry"), None),
        P(("pas", "qry"), None),
        P(("pas", "qry"), None, None),
        P(("pas", "qry"), None, None),
    )
    return jax.shard_map(
        on_device, mesh=mesh, in_specs=in_specs, out_specs=out_specs, check_vma=False
    )
```

```python
import functools
import math

import jax
import jax.numpy as jnp
from jax import lax
from jax.experimental import pallas as pl
from jax.experimental.pallas import tpu as pltpu
from jax.sharding import PartitionSpec as P

HQ = 32
HD = 128
Q_LEN = 64
CAP = 2
DEAD = 16.0
NEG = -1e30
SCALE = 1.0 / math.sqrt(HD)
SCALE2 = SCALE * math.log2(math.e)
BF = jnp.bfloat16
F32 = jnp.float32


def iota(shape, dim):
    return lax.broadcasted_iota(jnp.int32, shape, dim)


def dot(a, b, ca=1, cb=0):
    return lax.dot_general(a, b, (((ca,), (cb,)), ((), ())), preferred_element_type=F32)


def one(mask, dtype=BF):
    return jnp.where(mask, 1.0, 0.0).astype(dtype)


def slot_masks(ids, owners, n_local, plen):
    n_query, n_ret = ids.shape
    lanes = n_ret * plen
    own = lax.div(ids, n_local)
    loc = ids - own * n_local
    spread = one(iota((n_ret, lanes), 1) // plen == iota((n_ret, lanes), 0), F32)
    if plen > 1:
        own = dot(own.astype(F32), spread).astype(jnp.int32)
        loc = dot(loc.astype(F32), spread)
    else:
        loc = loc.astype(F32)
    before = one(
        (iota((lanes, lanes), 0) % plen == 0)
        & (iota((lanes, lanes), 0) // plen < iota((lanes, lanes), 1) // plen)
    )
    heads = one(iota((lanes, lanes), 0) % plen == 0)
    masks = []
    locals_ = []
    used = None
    for n in range(n_query):
        hit = iota((owners, lanes), 0) == own[n : n + 1]
        hit_b = one(hit)
        rank = dot(hit_b, before)
        if used is not None:
            rank = rank + used
        total = dot(hit_b, heads)
        used = total if used is None else used + total
        masks.append([one(hit & (rank == float(c)), F32) for c in range(CAP)])
        locals_.append(loc[n : n + 1])
    return masks, locals_


def request_kernel(owners, n_local, plen, ids_ref, req_ref):
    masks, locs = slot_masks(ids_ref[...], owners, n_local, 1)
    wanted = []
    for c in range(CAP):
        total = 0.0
        for mask, loc in zip(masks, locs):
            total = total + mask[c] * (loc + 1.0)
        wanted.append(jnp.sum(total, axis=1, keepdims=True))
    width = CAP * n_local * plen
    lane = iota((owners, width), 1)
    slot = lane // (n_local * plen)
    local = (lane % (n_local * plen)) // plen
    picked = jnp.where(slot == 0, wanted[0], wanted[1])
    req_ref[...] = one(picked == (local + 1).astype(F32), F32)


def prepare_kernel(
    owners,
    n_local,
    plen,
    len_ref,
    pk_ref,
    pv_ref,
    ids_ref,
    mask_ref,
    kv_ref,
    place_ref,
):
    rows = owners * CAP * plen
    width = CAP * n_local * plen
    chunk = CAP * plen
    row = iota((rows, width), 0)
    lane = iota((rows, width), 1)
    same = ((row % chunk) // plen == lane // (n_local * plen)) & (row % plen == lane % plen)
    lane_row = iota((1, width), 1)
    lane_m = (lane_row % (n_local * plen)) // plen
    live = jnp.zeros((1, width), jnp.int32)
    for m in range(n_local):
        live = jnp.where(lane_m == m, len_ref[m], live)
    live = lane_row % plen < live
    mask_ref[...] = one(same & live)
    kv_width = pk_ref.shape[2]
    half = n_local * plen
    for c in range(CAP):
        for m in range(n_local):
            at = c * half + m * plen
            kv_ref[at : at + plen, :kv_width] = pk_ref[m]
            kv_ref[at : at + plen, kv_width:] = pv_ref[m]

    n_query, n_ret = ids_ref.shape
    lanes = n_ret * plen
    masks, _ = slot_masks(ids_ref[...], owners, n_local, plen)
    row = iota((rows, CAP * owners), 0)
    lane = iota((rows, CAP * owners), 1)
    who = one((row // chunk == lane % owners) & ((row % chunk) // plen == lane // owners))
    same = iota((rows, lanes), 0) % plen == iota((rows, lanes), 1) % plen
    for n in range(n_query):
        asked = jnp.concatenate([m.astype(BF) for m in masks[n]], axis=0)
        place_ref[:, n * lanes : (n + 1) * lanes] = jnp.where(same, dot(who, asked), 0.0).astype(BF)


def owner_kernel(owners, plen, req_ref, mask_ref, kv_ref, send_ref, table_ref):
    rows, width = mask_ref.shape
    chunk = CAP * plen
    who = one(iota((rows, owners), 0) // chunk == iota((rows, owners), 1))
    spread = dot(who, req_ref[...].astype(BF))
    table = (spread * mask_ref[...].astype(F32)).astype(BF)
    table_ref[...] = table
    alive = dot(table, jnp.ones((width, HD), BF))
    fill = (1.0 - alive) * DEAD
    kv_width = kv_ref.shape[1] // 2
    sent = dot(table, kv_ref[...])
    for g in range(kv_width // HD):
        send_ref[:, g * HD : (g + 1) * HD] = (sent[:, g * HD : (g + 1) * HD] + fill).astype(BF)
    send_ref[:, kv_width:] = sent[:, kv_width:].astype(BF)


def attend_kernel(
    place_ref,
    recv_ref,
    q_ref,
    g_ref,
    sk_ref,
    sv_ref,
    dq_ref,
    dsk_ref,
    dsv_ref,
    terms_ref,
    kv_ref,
    out_ref,
):
    kv_width = sk_ref.shape[1]
    kv_heads = kv_width // HD
    group = HQ // kv_heads
    q_len = Q_LEN
    n_query = sk_ref.shape[0] // q_len
    lanes = place_ref.shape[1] // n_query
    wide = group * q_len
    kv_ref[...] = dot(place_ref[...], recv_ref[...], 0, 0).astype(BF)
    causal = iota((q_len, wide), 0) <= iota((q_len, wide), 1) % q_len
    for n in range(n_query):
        r0 = n * q_len
        k0 = n * lanes
        for g in range(kv_heads):
            col = g * HD
            vcol = kv_width + g * HD
            heads = [slice((g * group + x) * HD, (g * group + x + 1) * HD) for x in range(group)]
            q = jnp.concatenate([q_ref[r0 : r0 + q_len, h] for h in heads], axis=0)
            go = jnp.concatenate([g_ref[r0 : r0 + q_len, h] for h in heads], axis=0)
            pk = kv_ref[k0 : k0 + lanes, col : col + HD]
            keys = jnp.concatenate([pk, sk_ref[r0 : r0 + q_len, col : col + HD]], axis=0)
            values = jnp.concatenate(
                [kv_ref[k0 : k0 + lanes, vcol : vcol + HD], sv_ref[r0 : r0 + q_len, col : col + HD]],
                axis=0,
            )
            alive = pk.astype(F32) < 0.5 * DEAD
            alive = jnp.concatenate([alive] * (wide // HD), axis=1)
            s = dot(keys, q, 1, 1) * SCALE2
            s = jnp.concatenate(
                [jnp.where(alive, s[:lanes], NEG), jnp.where(causal, s[lanes:], NEG)], axis=0
            )
            e = jnp.exp2(s - jnp.max(s, axis=0, keepdims=True))
            p = e * (1.0 / jnp.sum(e, axis=0, keepdims=True))
            w = p.astype(BF)
            dp = dot(values, go, 1, 1)
            delta = jnp.sum(w.astype(F32) * dp, axis=0, keepdims=True)
            ds = (p * (dp - delta)).astype(BF)
            dv = dot(w, go)
            dk = dot(ds, q) * SCALE
            dq = (dot(ds, keys, 0, 0) * SCALE).astype(BF)
            for x in range(group):
                at_col = (g * group + x) * HD
                dq_ref[r0 : r0 + q_len, at_col : at_col + HD] = dq[x * q_len : (x + 1) * q_len]
            dsk_ref[r0 : r0 + q_len, col : col + HD] = dk[lanes:].astype(BF)
            dsv_ref[r0 : r0 + q_len, col : col + HD] = dv[lanes:].astype(BF)
            out_ref[k0 : k0 + lanes, col : col + HD] = dk[:lanes].astype(BF)
            out_ref[k0 : k0 + lanes, vcol : vcol + HD] = dv[:lanes].astype(BF)
    terms_ref[...] = dot(place_ref[...], out_ref[...]).astype(BF)


def owner_sum_kernel(table_ref, back_ref, sum_ref):
    total = dot(table_ref[...], back_ref[...], 0, 0)
    half = total.shape[0] // CAP
    sum_ref[...] = (total[:half] + total[half:]).astype(BF)


def final_kernel(parts_ref, gk_ref, gv_ref):
    total = jnp.sum(parts_ref[...].astype(F32), axis=0).astype(BF)
    n_out, plen, kv_width = gk_ref.shape
    for m in range(n_out):
        gk_ref[m] = total[m * plen : (m + 1) * plen, :kv_width]
        gv_ref[m] = total[m * plen : (m + 1) * plen, kv_width:]


VMEM = pl.BlockSpec(memory_space=pltpu.VMEM)
SMEM = pl.BlockSpec(memory_space=pltpu.SMEM)


def call(kernel, out_shape, in_specs, name, limit=16, scratch=(), cost=None):
    several = isinstance(out_shape, (list, tuple))
    return pl.pallas_call(
        kernel,
        out_shape=out_shape,
        in_specs=in_specs,
        out_specs=[VMEM] * len(out_shape) if several else VMEM,
        scratch_shapes=list(scratch),
        compiler_params=pltpu.CompilerParams(vmem_limit_bytes=limit * 2**20),
        cost_estimate=cost,
        name=name,
    )


def cost(flops, mib, exps=0):
    return pl.CostEstimate(
        flops=int(flops), bytes_accessed=int(mib * 2**20), transcendentals=int(exps)
    )


def on_device(
    queries,
    grad_out,
    suffix_keys,
    suffix_values,
    passage_keys,
    passage_values,
    passage_lengths,
    retrieved,
):
    owners = lax.axis_size("pas")
    groups = lax.axis_size("qry")
    n_local, plen, kv_width = passage_keys.shape
    n_query, n_ret = retrieved.shape
    lanes = n_ret * plen
    rows = owners * CAP * plen
    width = CAP * n_local * plen
    sds = jax.ShapeDtypeStruct
    dims = (owners, n_local, plen)

    def exchange(x):
        parts = x.reshape((owners, rows // owners, x.shape[1]))
        return lax.all_to_all(parts, "pas", split_axis=0, concat_axis=0, tiled=True).reshape(x.shape)

    request = call(
        functools.partial(request_kernel, *dims), sds((owners, width), F32), [VMEM], "request"
    )(retrieved)
    asked = lax.all_to_all(
        request.reshape(owners, 1, width), "pas", split_axis=0, concat_axis=0, tiled=True
    ).reshape(owners, width)

    mask, tables, place = call(
        functools.partial(prepare_kernel, *dims),
        [
            sds((rows, width), BF),
            sds((width, 2 * kv_width), BF),
            sds((rows, n_query * lanes), BF),
        ],
        [SMEM] + [VMEM] * 3,
        "prepare",
        cost=cost(1e8, 1),
    )(passage_lengths, passage_keys, passage_values, retrieved)
    send, table = call(
        functools.partial(owner_kernel, owners, plen),
        [sds((rows, 2 * kv_width), BF), sds((rows, width), BF)],
        [VMEM, VMEM, VMEM],
        "owner_gather",
    )(asked, mask, tables)
    recv = exchange(send)

    dq, dsk, dsv, terms = call(
        attend_kernel,
        [
            sds(queries.shape, BF),
            sds(suffix_keys.shape, BF),
            sds(suffix_values.shape, BF),
            sds((rows, 2 * kv_width), BF),
        ],
        [VMEM] * 6,
        "attend",
        limit=24,
        scratch=[pltpu.VMEM((n_query * lanes, 2 * kv_width), BF)] * 2,
    )(place, recv, queries, grad_out, suffix_keys, suffix_values)
    back = exchange(terms)

    sums = call(owner_sum_kernel, sds((n_local * plen, 2 * kv_width), BF), [VMEM] * 2, "owner_sum")(
        table, back
    )
    parts = lax.all_to_all(
        sums.reshape(groups, n_local // groups * plen, 2 * kv_width),
        "qry",
        split_axis=0,
        concat_axis=0,
        tiled=True,
    )
    out = sds((n_local // groups, plen, kv_width), BF)
    gk, gv = call(final_kernel, [out, out], [VMEM], "final_sum")(parts)
    return dq, dsk, dsv, gk, gv


def solution(mesh):
    in_specs = (
        P(("pas", "qry"), None),
        P(("pas", "qry"), None),
        P(("pas", "qry"), None),
        P(("pas", "qry"), None),
        P("pas", None, None),
        P("pas", None, None),
        P("pas"),
        P(("pas", "qry"), None),
    )
    out_specs = (
        P(("pas", "qry"), None),
        P(("pas", "qry"), None),
        P(("pas", "qry"), None),
        P(("pas", "qry"), None, None),
        P(("pas", "qry"), None, None),
    )
    return jax.shard_map(
        on_device, mesh=mesh, in_specs=in_specs, out_specs=out_specs, check_vma=False
    )
```

```python
import functools
import math

import jax
import jax.numpy as jnp
from jax import lax
from jax.experimental import pallas as pl
from jax.experimental.pallas import tpu as pltpu
from jax.sharding import PartitionSpec as P

HQ = 32
HD = 128
Q_LEN = 64
CAP = 2
DEAD = 16.0
NEG = -1e30
SCALE = 1.0 / math.sqrt(HD)
SCALE2 = SCALE * math.log2(math.e)
BF = jnp.bfloat16
F32 = jnp.float32


def iota(shape, dim):
    return lax.broadcasted_iota(jnp.int32, shape, dim)


def dot(a, b, ca=1, cb=0):
    return lax.dot_general(a, b, (((ca,), (cb,)), ((), ())), preferred_element_type=F32)


def one(mask, dtype=BF):
    return jnp.where(mask, 1.0, 0.0).astype(dtype)


def slots(ids, owners, n_local, spread):
    n_query, n_ret = ids.shape
    lanes = n_ret * spread
    own = lax.div(ids, n_local)
    loc = (ids - own * n_local).astype(F32)
    if spread > 1:
        copies = one(iota((n_ret, lanes), 1) // spread == iota((n_ret, lanes), 0), F32)
        own = dot(own.astype(F32), copies).astype(jnp.int32)
        loc = dot(loc, copies)
    owner = iota((owners, lanes), 0)
    hits = [owner == own[n : n + 1] for n in range(n_query)]
    locs = [loc[n : n + 1] for n in range(n_query)]
    low = functools.reduce(
        jnp.minimum, [jnp.where(h, x, float(n_local)) for h, x in zip(hits, locs)]
    )
    high = functools.reduce(jnp.maximum, [jnp.where(h, x, -1.0) for h, x in zip(hits, locs)])
    low = jnp.min(low, axis=1, keepdims=True)
    high = jnp.max(high, axis=1, keepdims=True)
    return low, jnp.where(high > low, high, -1.0), hits, locs


def request_kernel(owners, n_local, plen, ids_ref, req_ref):
    low, high, _, _ = slots(ids_ref[...], owners, n_local, 1)
    width = CAP * n_local * plen
    lane = iota((owners, width), 1)
    slot = lane // (n_local * plen)
    local = (lane % (n_local * plen)) // plen
    req_ref[...] = one(jnp.where(slot == 0, low, high) == local.astype(F32), F32)


def prepare_kernel(
    owners,
    n_local,
    plen,
    len_ref,
    pk_ref,
    pv_ref,
    ids_ref,
    mask_ref,
    kv_ref,
    place_ref,
):
    rows = owners * CAP * plen
    width = CAP * n_local * plen
    chunk = CAP * plen
    row = iota((rows, width), 0)
    lane = iota((rows, width), 1)
    same = ((row % chunk) // plen == lane // (n_local * plen)) & (row % plen == lane % plen)
    lane_row = iota((1, width), 1)
    lane_m = (lane_row % (n_local * plen)) // plen
    live = jnp.zeros((1, width), jnp.int32)
    for m in range(n_local):
        live = jnp.where(lane_m == m, len_ref[m], live)
    live = lane_row % plen < live
    mask_ref[...] = one(same & live)
    kv_width = pk_ref.shape[2]
    half = n_local * plen
    for c in range(CAP):
        for m in range(n_local):
            at = c * half + m * plen
            kv_ref[at : at + plen, :kv_width] = pk_ref[m]
            kv_ref[at : at + plen, kv_width:] = pv_ref[m]

    n_query, n_ret = ids_ref.shape
    lanes = n_ret * plen
    low, high, hits, locs = slots(ids_ref[...], owners, n_local, plen)
    row = iota((rows, CAP * owners), 0)
    lane = iota((rows, CAP * owners), 1)
    who = one((row // chunk == lane % owners) & ((row % chunk) // plen == lane // owners))
    same = iota((rows, lanes), 0) % plen == iota((rows, lanes), 1) % plen
    for n in range(n_query):
        asked = jnp.concatenate(
            [one(hits[n] & (locs[n] == picked)) for picked in (low, high)], axis=0
        )
        place_ref[:, n * lanes : (n + 1) * lanes] = jnp.where(same, dot(who, asked), 0.0).astype(BF)


def owner_kernel(owners, plen, req_ref, mask_ref, kv_ref, send_ref, table_ref):
    rows, width = mask_ref.shape
    chunk = CAP * plen
    who = one(iota((rows, owners), 0) // chunk == iota((rows, owners), 1))
    spread = dot(who, req_ref[...].astype(BF))
    table = (spread * mask_ref[...].astype(F32)).astype(BF)
    table_ref[...] = table
    alive = dot(table, jnp.ones((width, HD), BF))
    fill = (1.0 - alive) * DEAD
    kv_width = kv_ref.shape[1] // 2
    sent = dot(table, kv_ref[...])
    for g in range(kv_width // HD):
        send_ref[:, g * HD : (g + 1) * HD] = (sent[:, g * HD : (g + 1) * HD] + fill).astype(BF)
    send_ref[:, kv_width:] = sent[:, kv_width:].astype(BF)


def attend_kernel(
    place_ref,
    recv_ref,
    q_ref,
    g_ref,
    sk_ref,
    sv_ref,
    dq_ref,
    dsk_ref,
    dsv_ref,
    terms_ref,
    kv_ref,
    out_ref,
):
    kv_width = sk_ref.shape[1]
    kv_heads = kv_width // HD
    group = HQ // kv_heads
    q_len = Q_LEN
    n_query = sk_ref.shape[0] // q_len
    lanes = place_ref.shape[1] // n_query
    wide = group * q_len
    kv_ref[...] = dot(place_ref[...], recv_ref[...], 0, 0).astype(BF)
    causal = iota((q_len, wide), 0) <= iota((q_len, wide), 1) % q_len
    pairs = [(n, g) for n in range(n_query) for g in range(kv_heads)]

    def load(n, g):
        r0 = n * q_len
        k0 = n * lanes
        col = slice(g * HD, (g + 1) * HD)
        vcol = slice(kv_width + g * HD, kv_width + (g + 1) * HD)
        heads = [slice((g * group + x) * HD, (g * group + x + 1) * HD) for x in range(group)]
        q = jnp.concatenate([q_ref[r0 : r0 + q_len, h] for h in heads], axis=0)
        go = jnp.concatenate([g_ref[r0 : r0 + q_len, h] for h in heads], axis=0)
        keys = jnp.concatenate(
            [kv_ref[k0 : k0 + lanes, col], sk_ref[r0 : r0 + q_len, col]], axis=0
        )
        values = jnp.concatenate(
            [kv_ref[k0 : k0 + lanes, vcol], sv_ref[r0 : r0 + q_len, col]], axis=0
        )
        return q, go, keys, values

    def products(n, g):
        q, go, keys, values = load(n, g)
        return dot(keys, q, 1, 1), dot(values, go, 1, 1)

    def weigh(n, g, s, dp):
        pk = kv_ref[n * lanes : (n + 1) * lanes, g * HD : (g + 1) * HD]
        alive = pk.astype(F32) < 0.5 * DEAD
        alive = jnp.concatenate([alive] * (wide // HD), axis=1)
        s = s * SCALE2
        s = jnp.concatenate(
            [jnp.where(alive, s[:lanes], NEG), jnp.where(causal, s[lanes:], NEG)], axis=0
        )
        e = jnp.exp2(s - jnp.max(s, axis=0, keepdims=True))
        p = e * (1.0 / jnp.sum(e, axis=0, keepdims=True))
        w = p.astype(BF)
        delta = jnp.sum(w.astype(F32) * dp, axis=0, keepdims=True)
        return w, (p * (dp - delta)).astype(BF)

    def store(n, g, w, ds):
        q, go, keys, _ = load(n, g)
        r0 = n * q_len
        k0 = n * lanes
        col = slice(g * HD, (g + 1) * HD)
        vcol = slice(kv_width + g * HD, kv_width + (g + 1) * HD)
        dv = dot(w, go)
        dk = dot(ds, q) * SCALE
        dq = (dot(ds, keys, 0, 0) * SCALE).astype(BF)
        for x in range(group):
            at = (g * group + x) * HD
            dq_ref[r0 : r0 + q_len, at : at + HD] = dq[x * q_len : (x + 1) * q_len]
        dsk_ref[r0 : r0 + q_len, col] = dk[lanes:].astype(BF)
        dsv_ref[r0 : r0 + q_len, col] = dv[lanes:].astype(BF)
        out_ref[k0 : k0 + lanes, col] = dk[:lanes].astype(BF)
        out_ref[k0 : k0 + lanes, vcol] = dv[:lanes].astype(BF)

    for a in range(0, len(pairs), 2):
        two = pairs[a : a + 2]
        both = [products(*pair) for pair in two]
        both = [weigh(*pair, *x) for pair, x in zip(two, both)]
        for pair, x in zip(two, both):
            store(*pair, *x)
    terms_ref[...] = dot(place_ref[...], out_ref[...]).astype(BF)


def owner_sum_kernel(table_ref, back_ref, sum_ref):
    total = dot(table_ref[...], back_ref[...], 0, 0)
    half = total.shape[0] // CAP
    sum_ref[...] = (total[:half] + total[half:]).astype(BF)


def final_kernel(parts_ref, gk_ref, gv_ref):
    total = jnp.sum(parts_ref[...].astype(F32), axis=0).astype(BF)
    n_out, plen, kv_width = gk_ref.shape
    for m in range(n_out):
        gk_ref[m] = total[m * plen : (m + 1) * plen, :kv_width]
        gv_ref[m] = total[m * plen : (m + 1) * plen, kv_width:]


VMEM = pl.BlockSpec(memory_space=pltpu.VMEM)
SMEM = pl.BlockSpec(memory_space=pltpu.SMEM)


def call(kernel, out_shape, in_specs, name, limit=16, scratch=(), cost=None):
    several = isinstance(out_shape, (list, tuple))
    return pl.pallas_call(
        kernel,
        out_shape=out_shape,
        in_specs=in_specs,
        out_specs=[VMEM] * len(out_shape) if several else VMEM,
        scratch_shapes=list(scratch),
        compiler_params=pltpu.CompilerParams(vmem_limit_bytes=limit * 2**20),
        cost_estimate=cost,
        name=name,
    )


def cost(flops, mib, exps=0):
    return pl.CostEstimate(
        flops=int(flops), bytes_accessed=int(mib * 2**20), transcendentals=int(exps)
    )


def on_device(
    queries,
    grad_out,
    suffix_keys,
    suffix_values,
    passage_keys,
    passage_values,
    passage_lengths,
    retrieved,
):
    owners = lax.axis_size("pas")
    groups = lax.axis_size("qry")
    n_local, plen, kv_width = passage_keys.shape
    n_query, n_ret = retrieved.shape
    lanes = n_ret * plen
    rows = owners * CAP * plen
    width = CAP * n_local * plen
    sds = jax.ShapeDtypeStruct
    dims = (owners, n_local, plen)

    def exchange(x):
        parts = x.reshape((owners, rows // owners, x.shape[1]))
        return lax.all_to_all(parts, "pas", split_axis=0, concat_axis=0, tiled=True).reshape(x.shape)

    request = call(
        functools.partial(request_kernel, *dims), sds((owners, width), F32), [VMEM], "request"
    )(retrieved)
    asked = lax.all_to_all(
        request.reshape(owners, 1, width), "pas", split_axis=0, concat_axis=0, tiled=True
    ).reshape(owners, width)

    mask, tables, place = call(
        functools.partial(prepare_kernel, *dims),
        [
            sds((rows, width), BF),
            sds((width, 2 * kv_width), BF),
            sds((rows, n_query * lanes), BF),
        ],
        [SMEM] + [VMEM] * 3,
        "prepare",
        cost=cost(1e8, 1),
    )(passage_lengths, passage_keys, passage_values, retrieved)
    send, table = call(
        functools.partial(owner_kernel, owners, plen),
        [sds((rows, 2 * kv_width), BF), sds((rows, width), BF)],
        [VMEM, VMEM, VMEM],
        "owner_gather",
    )(asked, mask, tables)
    recv = exchange(send)

    dq, dsk, dsv, terms = call(
        attend_kernel,
        [
            sds(queries.shape, BF),
            sds(suffix_keys.shape, BF),
            sds(suffix_values.shape, BF),
            sds((rows, 2 * kv_width), BF),
        ],
        [VMEM] * 6,
        "attend",
        limit=24,
        scratch=[pltpu.VMEM((n_query * lanes, 2 * kv_width), BF)] * 2,
    )(place, recv, queries, grad_out, suffix_keys, suffix_values)
    back = exchange(terms)

    sums = call(owner_sum_kernel, sds((n_local * plen, 2 * kv_width), BF), [VMEM] * 2, "owner_sum")(
        table, back
    )
    parts = lax.all_to_all(
        sums.reshape(groups, n_local // groups * plen, 2 * kv_width),
        "qry",
        split_axis=0,
        concat_axis=0,
        tiled=True,
    )
    out = sds((n_local // groups, plen, kv_width), BF)
    gk, gv = call(final_kernel, [out, out], [VMEM], "final_sum")(parts)
    return dq, dsk, dsv, gk, gv


def solution(mesh):
    in_specs = (
        P(("pas", "qry"), None),
        P(("pas", "qry"), None),
        P(("pas", "qry"), None),
        P(("pas", "qry"), None),
        P("pas", None, None),
        P("pas", None, None),
        P("pas"),
        P(("pas", "qry"), None),
    )
    out_specs = (
        P(("pas", "qry"), None),
        P(("pas", "qry"), None),
        P(("pas", "qry"), None),
        P(("pas", "qry"), None, None),
        P(("pas", "qry"), None, None),
    )
    return jax.shard_map(
        on_device, mesh=mesh, in_specs=in_specs, out_specs=out_specs, check_vma=False
    )
```

```python
import functools
import math

import jax
import jax.numpy as jnp
from jax import lax
from jax.experimental import pallas as pl
from jax.experimental.pallas import tpu as pltpu
from jax.sharding import PartitionSpec as P

HQ = 32
HD = 128
Q_LEN = 64
CAP = 2
DEAD = 16.0
NEG = -1e30
SCALE = 1.0 / math.sqrt(HD)
SCALE2 = SCALE * math.log2(math.e)
BF = jnp.bfloat16
F32 = jnp.float32


def iota(shape, dim):
    return lax.broadcasted_iota(jnp.int32, shape, dim)


def dot(a, b, ca=1, cb=0):
    return lax.dot_general(a, b, (((ca,), (cb,)), ((), ())), preferred_element_type=F32)


def one(mask, dtype=BF):
    return jnp.where(mask, 1.0, 0.0).astype(dtype)


def slots(ids, owners, n_local, spread):
    n_query, n_ret = ids.shape
    lanes = n_ret * spread
    own = lax.div(ids, n_local)
    loc = (ids - own * n_local).astype(F32)
    if spread > 1:
        copies = one(iota((n_ret, lanes), 1) // spread == iota((n_ret, lanes), 0), F32)
        own = dot(own.astype(F32), copies).astype(jnp.int32)
        loc = dot(loc, copies)
    owner = iota((owners, lanes), 0)
    hits = [owner == own[n : n + 1] for n in range(n_query)]
    locs = [loc[n : n + 1] for n in range(n_query)]
    low = functools.reduce(
        jnp.minimum, [jnp.where(h, x, float(n_local)) for h, x in zip(hits, locs)]
    )
    high = functools.reduce(jnp.maximum, [jnp.where(h, x, -1.0) for h, x in zip(hits, locs)])
    low = jnp.min(low, axis=1, keepdims=True)
    high = jnp.max(high, axis=1, keepdims=True)
    return low, jnp.where(high > low, high, -1.0), hits, locs


def request_kernel(owners, n_local, plen, ids_ref, req_ref):
    low, high, _, _ = slots(ids_ref[...], owners, n_local, 1)
    width = CAP * n_local * plen
    lane = iota((owners, width), 1)
    slot = lane // (n_local * plen)
    local = (lane % (n_local * plen)) // plen
    req_ref[...] = one(jnp.where(slot == 0, low, high) == local.astype(F32), F32)


def prepare_kernel(
    owners,
    n_local,
    plen,
    len_ref,
    pk_ref,
    pv_ref,
    ids_ref,
    mask_ref,
    kv_ref,
    place_ref,
    take_ref,
):
    rows = owners * CAP * plen
    width = CAP * n_local * plen
    chunk = CAP * plen
    row = iota((rows, width), 0)
    lane = iota((rows, width), 1)
    same = ((row % chunk) // plen == lane // (n_local * plen)) & (row % plen == lane % plen)
    lane_row = iota((1, width), 1)
    lane_m = (lane_row % (n_local * plen)) // plen
    live = jnp.zeros((1, width), jnp.int32)
    for m in range(n_local):
        live = jnp.where(lane_m == m, len_ref[m], live)
    live = lane_row % plen < live
    mask_ref[...] = one(same & live)
    kv_width = pk_ref.shape[2]
    half = n_local * plen
    for c in range(CAP):
        for m in range(n_local):
            at = c * half + m * plen
            kv_ref[at : at + plen, :kv_width] = pk_ref[m]
            kv_ref[at : at + plen, kv_width:] = pv_ref[m]

    n_query, n_ret = ids_ref.shape
    lanes = n_ret * plen
    low, high, hits, locs = slots(ids_ref[...], owners, n_local, plen)
    row = iota((rows, CAP * owners), 0)
    lane = iota((rows, CAP * owners), 1)
    who = one((row // chunk == lane % owners) & ((row % chunk) // plen == lane // owners))
    same = iota((rows, lanes), 0) % plen == iota((rows, lanes), 1) % plen
    for n in range(n_query):
        asked = jnp.concatenate(
            [one(hits[n] & (locs[n] == picked)) for picked in (low, high)], axis=0
        )
        place = jnp.where(same, dot(who, asked), 0.0)
        place_ref[:, n * lanes : (n + 1) * lanes] = place.astype(BF)
        take_ref[n * lanes : (n + 1) * lanes] = place.T.astype(BF)


def owner_kernel(owners, plen, req_ref, mask_ref, kv_ref, send_ref, table_ref):
    rows, width = mask_ref.shape
    chunk = CAP * plen
    who = one(iota((rows, owners), 0) // chunk == iota((rows, owners), 1))
    spread = dot(who, req_ref[...].astype(BF))
    table = (spread * mask_ref[...].astype(F32)).astype(BF)
    table_ref[...] = table
    alive = dot(table, jnp.ones((width, HD), BF))
    fill = (1.0 - alive) * DEAD
    kv_width = kv_ref.shape[1] // 2
    sent = dot(table, kv_ref[...])
    for g in range(kv_width // HD):
        send_ref[:, g * HD : (g + 1) * HD] = (sent[:, g * HD : (g + 1) * HD] + fill).astype(BF)
    send_ref[:, kv_width:] = sent[:, kv_width:].astype(BF)


def attend_kernel(
    place_ref,
    take_ref,
    recv_ref,
    q_ref,
    g_ref,
    sk_ref,
    sv_ref,
    dq_ref,
    dsk_ref,
    dsv_ref,
    terms_ref,
    kv_ref,
    out_ref,
):
    kv_width = sk_ref.shape[1]
    kv_heads = kv_width // HD
    group = HQ // kv_heads
    q_len = Q_LEN
    n_query = sk_ref.shape[0] // q_len
    lanes = place_ref.shape[1] // n_query
    wide = group * q_len
    kv_ref[...] = dot(take_ref[...], recv_ref[...]).astype(BF)
    causal = iota((q_len, wide), 0) <= iota((q_len, wide), 1) % q_len
    pairs = [(n, g) for n in range(n_query) for g in range(kv_heads)]

    def load(n, g):
        r0 = n * q_len
        k0 = n * lanes
        col = slice(g * HD, (g + 1) * HD)
        vcol = slice(kv_width + g * HD, kv_width + (g + 1) * HD)
        heads = [slice((g * group + x) * HD, (g * group + x + 1) * HD) for x in range(group)]
        q = jnp.concatenate([q_ref[r0 : r0 + q_len, h] for h in heads], axis=0)
        go = jnp.concatenate([g_ref[r0 : r0 + q_len, h] for h in heads], axis=0)
        keys = jnp.concatenate(
            [kv_ref[k0 : k0 + lanes, col], sk_ref[r0 : r0 + q_len, col]], axis=0
        )
        values = jnp.concatenate(
            [kv_ref[k0 : k0 + lanes, vcol], sv_ref[r0 : r0 + q_len, col]], axis=0
        )
        return q, go, keys, values

    def products(n, g):
        q, go, keys, values = load(n, g)
        return dot(keys, q, 1, 1), dot(values, go, 1, 1)

    def weigh(n, g, s, dp):
        pk = kv_ref[n * lanes : (n + 1) * lanes, g * HD : (g + 1) * HD]
        alive = pk.astype(F32) < 0.5 * DEAD
        alive = jnp.concatenate([alive] * (wide // HD), axis=1)
        s = s * SCALE2
        s = jnp.concatenate(
            [jnp.where(alive, s[:lanes], NEG), jnp.where(causal, s[lanes:], NEG)], axis=0
        )
        e = jnp.exp2(s - jnp.max(s, axis=0, keepdims=True))
        p = e * (1.0 / jnp.sum(e, axis=0, keepdims=True))
        w = p.astype(BF)
        delta = jnp.sum(w.astype(F32) * dp, axis=0, keepdims=True)
        return w, (p * (dp - delta)).astype(BF)

    def store(n, g, w, ds):
        q, go, keys, _ = load(n, g)
        r0 = n * q_len
        k0 = n * lanes
        col = slice(g * HD, (g + 1) * HD)
        vcol = slice(kv_width + g * HD, kv_width + (g + 1) * HD)
        dv = dot(w, go)
        dk = dot(ds, q) * SCALE
        dq = (dot(ds, keys, 0, 0) * SCALE).astype(BF)
        for x in range(group):
            at = (g * group + x) * HD
            dq_ref[r0 : r0 + q_len, at : at + HD] = dq[x * q_len : (x + 1) * q_len]
        dsk_ref[r0 : r0 + q_len, col] = dk[lanes:].astype(BF)
        dsv_ref[r0 : r0 + q_len, col] = dv[lanes:].astype(BF)
        out_ref[k0 : k0 + lanes, col] = dk[:lanes].astype(BF)
        out_ref[k0 : k0 + lanes, vcol] = dv[:lanes].astype(BF)

    for a in range(0, len(pairs), 2):
        two = pairs[a : a + 2]
        both = [products(*pair) for pair in two]
        both = [weigh(*pair, *x) for pair, x in zip(two, both)]
        for pair, x in zip(two, both):
            store(*pair, *x)
    terms_ref[...] = dot(place_ref[...], out_ref[...]).astype(BF)


def owner_sum_kernel(table_ref, back_ref, sum_ref):
    total = dot(table_ref[...], back_ref[...], 0, 0)
    half = total.shape[0] // CAP
    sum_ref[...] = (total[:half] + total[half:]).astype(BF)


def final_kernel(parts_ref, gk_ref, gv_ref):
    total = jnp.sum(parts_ref[...].astype(F32), axis=0).astype(BF)
    n_out, plen, kv_width = gk_ref.shape
    for m in range(n_out):
        gk_ref[m] = total[m * plen : (m + 1) * plen, :kv_width]
        gv_ref[m] = total[m * plen : (m + 1) * plen, kv_width:]


VMEM = pl.BlockSpec(memory_space=pltpu.VMEM)
SMEM = pl.BlockSpec(memory_space=pltpu.SMEM)


def call(kernel, out_shape, in_specs, name, limit=16, scratch=(), cost=None):
    several = isinstance(out_shape, (list, tuple))
    return pl.pallas_call(
        kernel,
        out_shape=out_shape,
        in_specs=in_specs,
        out_specs=[VMEM] * len(out_shape) if several else VMEM,
        scratch_shapes=list(scratch),
        compiler_params=pltpu.CompilerParams(vmem_limit_bytes=limit * 2**20),
        cost_estimate=cost,
        name=name,
    )


def cost(flops, mib, exps=0):
    return pl.CostEstimate(
        flops=int(flops), bytes_accessed=int(mib * 2**20), transcendentals=int(exps)
    )


def on_device(
    queries,
    grad_out,
    suffix_keys,
    suffix_values,
    passage_keys,
    passage_values,
    passage_lengths,
    retrieved,
):
    owners = lax.axis_size("pas")
    groups = lax.axis_size("qry")
    n_local, plen, kv_width = passage_keys.shape
    n_query, n_ret = retrieved.shape
    lanes = n_ret * plen
    rows = owners * CAP * plen
    width = CAP * n_local * plen
    sds = jax.ShapeDtypeStruct
    dims = (owners, n_local, plen)

    def exchange(x):
        parts = x.reshape((owners, rows // owners, x.shape[1]))
        return lax.all_to_all(parts, "pas", split_axis=0, concat_axis=0, tiled=True).reshape(x.shape)

    request = call(
        functools.partial(request_kernel, *dims), sds((owners, width), F32), [VMEM], "request"
    )(retrieved)
    asked = lax.all_to_all(
        request.reshape(owners, 1, width), "pas", split_axis=0, concat_axis=0, tiled=True
    ).reshape(owners, width)

    mask, tables, place, take = call(
        functools.partial(prepare_kernel, *dims),
        [
            sds((rows, width), BF),
            sds((width, 2 * kv_width), BF),
            sds((rows, n_query * lanes), BF),
            sds((n_query * lanes, rows), BF),
        ],
        [SMEM] + [VMEM] * 3,
        "prepare",
        cost=cost(1e8, 1),
    )(passage_lengths, passage_keys, passage_values, retrieved)
    send, table = call(
        functools.partial(owner_kernel, owners, plen),
        [sds((rows, 2 * kv_width), BF), sds((rows, width), BF)],
        [VMEM, VMEM, VMEM],
        "owner_gather",
    )(asked, mask, tables)
    recv = exchange(send)

    dq, dsk, dsv, terms = call(
        attend_kernel,
        [
            sds(queries.shape, BF),
            sds(suffix_keys.shape, BF),
            sds(suffix_values.shape, BF),
            sds((rows, 2 * kv_width), BF),
        ],
        [VMEM] * 7,
        "attend",
        limit=24,
        scratch=[pltpu.VMEM((n_query * lanes, 2 * kv_width), BF)] * 2,
    )(place, take, recv, queries, grad_out, suffix_keys, suffix_values)
    back = exchange(terms)

    sums = call(owner_sum_kernel, sds((n_local * plen, 2 * kv_width), BF), [VMEM] * 2, "owner_sum")(
        table, back
    )
    parts = lax.all_to_all(
        sums.reshape(groups, n_local // groups * plen, 2 * kv_width),
        "qry",
        split_axis=0,
        concat_axis=0,
        tiled=True,
    )
    out = sds((n_local // groups, plen, kv_width), BF)
    gk, gv = call(final_kernel, [out, out], [VMEM], "final_sum")(parts)
    return dq, dsk, dsv, gk, gv


def solution(mesh):
    in_specs = (
        P(("pas", "qry"), None),
        P(("pas", "qry"), None),
        P(("pas", "qry"), None),
        P(("pas", "qry"), None),
        P("pas", None, None),
        P("pas", None, None),
        P("pas"),
        P(("pas", "qry"), None),
    )
    out_specs = (
        P(("pas", "qry"), None),
        P(("pas", "qry"), None),
        P(("pas", "qry"), None),
        P(("pas", "qry"), None, None),
        P(("pas", "qry"), None, None),
    )
    return jax.shard_map(
        on_device, mesh=mesh, in_specs=in_specs, out_specs=out_specs, check_vma=False
    )
```
